128 devices in a mesh: seq: 32 (over x, y_hi, z), dp: 4 (over y_lo, core).
Axes of the slice: x: 4, y: 4 (y_hi: 2, y_lo: 2; y = y_hi * 2 + y_lo), z: 4, core: 2. Of those that a mesh axis runs over, the one named last changes fastest.
Arguments:
- query: bfloat16 [4, 16384, 2048], P('dp', 'seq'), may hold values from -100 to 100
- key: bfloat16 [4, 16384, 2048], P('dp', 'seq'), may hold values from -6 to 6
- value: bfloat16 [4, 16384, 2048], P('dp', 'seq'), may hold values from -6 to 6
- grad_ctx: bfloat16 [4, 16384, 2048], P('dp', 'seq'), may hold values from -6 to 6
- proj_key: bfloat16 [512, 16384], P(None, 'seq'), may hold values from -0.046875 to 0.046875
- proj_value: bfloat16 [512, 16384], P(None, 'seq'), may hold values from -0.046875 to 0.046875
Outputs:
- grad_query: bfloat16 [4, 16384, 2048], P('dp', 'seq')
- grad_key: bfloat16 [4, 16384, 2048], P('dp', 'seq')
- grad_value: bfloat16 [4, 16384, 2048], P('dp', 'seq')
- grad_proj_key: bfloat16 [512, 16384], P('dp', 'seq')
- grad_proj_value: bfloat16 [512, 16384], P('dp', 'seq')
The draws below stay inside these ranges and needn't reach their ends.
All inputs are finite; a program needn't handle non-finite values.
Results may differ from the reference program's by a relative error of at most 0.034.
The reference program's roundings to bfloat16 on the way count: a program that leaves them out, or rounds other values in their place, can miss the bound.
Values may be sent and summed in bfloat16 or wider, within the bound.
No kernel may reach another device: no remote copies, remote signals or barrier semaphores. Data moves between devices by JAX's collectives and lax.ppermute only.
A program may use at most 128 MiB of HBM per device.

```python
import jax
import jax.numpy as jnp
from jax import lax

H = 16
HEAD_DIM = 128
KP = 512
HD = 2048
SEQ_LEN = 16384
N_DP = 4


def draw_query(key, part):
    key = jax.random.fold_in(key, 5)
    first = jax.random.fold_in(key, 0)
    shape = (N_DP, SEQ_LEN, HD)
    values = jnp.clip(jax.random.normal(first, shape, jnp.float32), -5.0, 5.0)
    return values.astype(jnp.bfloat16)


def shard_levels(rng, extent, shards, least, top_value):
    def one(axis_at, parts):
        steps = jax.random.uniform(jax.random.fold_in(jax.random.fold_in(rng, 6), axis_at), (parts,), jnp.float32, least / len(shards), top_value / len(shards))
        return jnp.repeat(jnp.exp(steps), extent[axis_at] // parts).reshape((-1,) + (1,) * (len(extent) - axis_at - 1))

    factor_of = one(*shards[0])
    for cut in shards[1:]:
        factor_of = factor_of * one(*cut)
    return factor_of


def noise(rng, extent, width, reach, cuts=(), dtype=jnp.bfloat16):
    level = shard_levels(rng, extent, cuts, -0.22, 0.18) if cuts else 1.0
    result = jax.random.normal(rng, extent, jnp.float32) * width * level
    return jnp.minimum(jnp.maximum(result, -reach), reach).astype(dtype)


def setup_inputs(seed: int = 0) -> dict:
    key_list = jax.random.split(jax.random.key(seed), 7)
    return {
        "query": draw_query(jax.random.fold_in(key_list[6], 71), 0),
        "key": noise(key_list[1], (N_DP, SEQ_LEN, HD), 1.0, 6.0, ((0, 4), (1, 32))),
        "value": noise(key_list[2], (N_DP, SEQ_LEN, HD), 1.0, 6.0, ((0, 4), (1, 32))),
        "grad_ctx": noise(key_list[3], (N_DP, SEQ_LEN, HD), 1.0, 6.0, ((0, 4), (1, 32))),
        "proj_key": noise(key_list[4], (KP, SEQ_LEN), SEQ_LEN ** -0.5, 0.046875, ((1, 32),)),
        "proj_value": noise(key_list[5], (KP, SEQ_LEN), SEQ_LEN ** -0.5, 0.046875, ((1, 32),)),
    }


def head_pass(q, g, kp, vp):
    scale = HEAD_DIM ** -0.5
    hd_total = q.shape[1]
    rows = q.shape[0]
    gq = jnp.zeros((rows, hd_total), jnp.bfloat16)
    dkp = jnp.zeros((kp.shape[0], hd_total), jnp.float32)
    dvp = jnp.zeros((kp.shape[0], hd_total), jnp.float32)

    def per_head(h, carry):
        gq, dkp, dvp = carry
        start = (h * HEAD_DIM).astype(jnp.int32)
        q_head = lax.dynamic_slice_in_dim(q, start, HEAD_DIM, 1)
        g_head = lax.dynamic_slice_in_dim(g, start, HEAD_DIM, 1)
        kp_head = lax.dynamic_slice_in_dim(kp, start, HEAD_DIM, 1)
        vp_head = lax.dynamic_slice_in_dim(vp, start, HEAD_DIM, 1)
        scores = lax.dot_general(q_head, kp_head, (((1,), (1,)), ((), ())), preferred_element_type=jnp.float32) * scale
        probs = jax.nn.softmax(scores, axis=-1)
        probs_low = probs.astype(jnp.bfloat16)
        grad_probs = lax.dot_general(g_head, vp_head, (((1,), (1,)), ((), ())), preferred_element_type=jnp.float32)
        delta = jnp.sum(probs * grad_probs, axis=-1, keepdims=True)
        grad_scores = (probs * (grad_probs - delta) * scale).astype(jnp.bfloat16)
        gq_head = jnp.dot(grad_scores, kp_head, preferred_element_type=jnp.float32).astype(jnp.bfloat16)
        dkp_head = lax.dot_general(grad_scores, q_head, (((0,), (0,)), ((), ())), preferred_element_type=jnp.float32)
        dvp_head = lax.dot_general(probs_low, g_head, (((0,), (0,)), ((), ())), preferred_element_type=jnp.float32)
        gq = lax.dynamic_update_slice_in_dim(gq, gq_head, start, 1)
        dkp = lax.dynamic_update_slice_in_dim(dkp, dkp_head, start, 1)
        dvp = lax.dynamic_update_slice_in_dim(dvp, dvp_head, start, 1)
        return gq, dkp, dvp

    return lax.fori_loop(0, H, per_head, (gq, dkp, dvp))


def reference(query, key, value, grad_ctx, proj_key, proj_value):
    gq_all = []
    gk_all = []
    gv_all = []
    sum_pk = jnp.zeros((KP, SEQ_LEN), jnp.float32)
    sum_pv = jnp.zeros((KP, SEQ_LEN), jnp.float32)
    for rep in range(N_DP):
        q = query[rep]
        k = key[rep]
        v = value[rep]
        g = grad_ctx[rep]
        kp = jnp.dot(proj_key, k, preferred_element_type=jnp.float32).astype(jnp.bfloat16)
        vp = jnp.dot(proj_value, v, preferred_element_type=jnp.float32).astype(jnp.bfloat16)
        gq, dkp, dvp = head_pass(q, g, kp, vp)
        dkp = dkp.astype(jnp.bfloat16)
        dvp = dvp.astype(jnp.bfloat16)
        gk = lax.dot_general(proj_key, dkp, (((0,), (0,)), ((), ())), preferred_element_type=jnp.float32).astype(jnp.bfloat16)
        gv = lax.dot_general(proj_value, dvp, (((0,), (0,)), ((), ())), preferred_element_type=jnp.float32).astype(jnp.bfloat16)
        sum_pk = sum_pk + lax.dot_general(dkp, k, (((1,), (1,)), ((), ())), preferred_element_type=jnp.float32)
        sum_pv = sum_pv + lax.dot_general(dvp, v, (((1,), (1,)), ((), ())), preferred_element_type=jnp.float32)
        gq_all.append(gq)
        gk_all.append(gk)
        gv_all.append(gv)
    return (jnp.stack(gq_all), jnp.stack(gk_all), jnp.stack(gv_all), sum_pk.astype(jnp.bfloat16), sum_pv.astype(jnp.bfloat16))
```

```python
import functools

import jax
import jax.numpy as jnp
from jax import lax
from jax.experimental import pallas as pl
from jax.experimental.pallas import tpu as pltpu
from jax.sharding import PartitionSpec as P

H = 16
HEAD_DIM = 128
SCALE = HEAD_DIM ** (-0.5)
N_SEQ = 32
N_DP = 4
F32 = jnp.float32
BF16 = jnp.bfloat16


def dot(a, b, dims):
    return lax.dot_general(a, b, (dims, ((), ())), preferred_element_type=F32)


def probs_kernel(q_ref, g_ref, kp_ref, dvp_ref, top_ref, inv_ref):
    scores = dot(kp_ref[...], q_ref[...], ((1,), (1,))) * SCALE
    top = jnp.max(scores, axis=0, keepdims=True)
    e = jnp.exp(scores - top)
    inv = 1.0 / jnp.sum(e, axis=0, keepdims=True)
    probs_low = (e * inv).astype(BF16)
    dvp_ref[...] = dot(probs_low, g_ref[...], ((1,), (0,))).astype(BF16)
    top_ref[0] = top
    inv_ref[0] = inv


def scores_kernel(q_ref, g_ref, kp_ref, vp_ref, top_ref, inv_ref, gq_ref, dkp_ref):
    scores = dot(kp_ref[...], q_ref[...], ((1,), (1,))) * SCALE
    probs = jnp.exp(scores - top_ref[0]) * inv_ref[0]
    grad_probs = dot(vp_ref[...], g_ref[...], ((1,), (1,)))
    delta = jnp.sum(probs * grad_probs, axis=0, keepdims=True)
    grad_scores = (probs * (grad_probs - delta) * SCALE).astype(BF16)
    dkp_ref[...] = dot(grad_scores, q_ref[...], ((1,), (0,))).astype(BF16)
    gq_t = dot(kp_ref[...], grad_scores, ((0,), (0,)))
    gq_ref[...] = gq_t.T.astype(BF16)


def head_block(rows):
    return pl.BlockSpec((rows, HEAD_DIM), lambda h: (0, h))


def stat_block(rows):
    return pl.BlockSpec((1, 1, rows), lambda h: (h, 0, 0))


def probs_call(q, g, kp):
    rows, feats = q.shape
    n = kp.shape[0]
    stat = jax.ShapeDtypeStruct((H, 1, rows), F32)
    return pl.pallas_call(
        probs_kernel,
        grid=(H,),
        in_specs=[head_block(rows), head_block(rows), head_block(n)],
        out_specs=[head_block(n), stat_block(rows), stat_block(rows)],
        out_shape=[jax.ShapeDtypeStruct((n, feats), BF16), stat, stat],
        compiler_params=pltpu.CompilerParams(vmem_limit_bytes=40 * 2**20),
        cost_estimate=pl.CostEstimate(
            flops=4 * rows * n * feats, bytes_accessed=8 * rows * feats, transcendentals=H * rows * n
        ),
    )(q, g, kp)


def scores_call(q, g, kp, vp, top, inv):
    rows, feats = q.shape
    n = kp.shape[0]
    return pl.pallas_call(
        scores_kernel,
        grid=(H,),
        in_specs=[
            head_block(rows),
            head_block(rows),
            head_block(n),
            head_block(n),
            stat_block(rows),
            stat_block(rows),
        ],
        out_specs=[head_block(rows), head_block(n)],
        out_shape=[
            jax.ShapeDtypeStruct((rows, feats), BF16),
            jax.ShapeDtypeStruct((n, feats), BF16),
        ],
        compiler_params=pltpu.CompilerParams(vmem_limit_bytes=40 * 2**20),
        cost_estimate=pl.CostEstimate(
            flops=8 * rows * n * feats, bytes_accessed=12 * rows * feats, transcendentals=H * rows * n
        ),
    )(q, g, kp, vp, top, inv)


def back_kernel(p_ref, d_ref, o_ref):
    o_ref[...] = dot(p_ref[...], d_ref[...], ((0,), (0,))).astype(BF16)


def back_call(proj, d):
    n, rows = proj.shape
    feats = d.shape[1]
    wide = 512
    return pl.pallas_call(
        back_kernel,
        grid=(feats // wide,),
        in_specs=[
            pl.BlockSpec((n, rows), lambda i: (0, 0)),
            pl.BlockSpec((n, wide), lambda i: (0, i)),
        ],
        out_specs=pl.BlockSpec((rows, wide), lambda i: (0, i)),
        out_shape=jax.ShapeDtypeStruct((rows, feats), BF16),
        compiler_params=pltpu.CompilerParams(vmem_limit_bytes=40 * 2**20),
        cost_estimate=pl.CostEstimate(
            flops=2 * rows * n * feats, bytes_accessed=4 * rows * feats, transcendentals=0
        ),
    )(proj, d)


def all_sum(part):
    n, feats = part.shape
    own = n // N_SEQ
    got = lax.all_to_all(part.reshape(N_SEQ, own, feats), "seq", 0, 0)
    total = jnp.sum(got.astype(F32), axis=0).astype(BF16)
    full = lax.all_to_all(jnp.broadcast_to(total[None], (N_SEQ, own, feats)), "seq", 0, 0)
    return full.reshape(n, feats)


def dp_sum(term):
    n, rows = term.shape
    got = lax.all_to_all(term.reshape(N_DP, n // N_DP, rows), "dp", 0, 0)
    return jnp.sum(got.astype(F32), axis=0).astype(BF16)


def body(query, key, value, grad_ctx, proj_key, proj_value):
    q, k, v, g = query[0], key[0], value[0], grad_ctx[0]
    kp = all_sum(dot(proj_key, k, ((1,), (0,))).astype(BF16))
    vp = all_sum(dot(proj_value, v, ((1,), (0,))).astype(BF16))
    dvp_part, top, inv = probs_call(q, g, kp)
    dvp = all_sum(dvp_part)
    gq, dkp_part = scores_call(q, g, kp, vp, top, inv)
    dkp = all_sum(dkp_part)
    sum_v = dp_sum(dot(dvp, v, ((1,), (1,))).astype(BF16))
    sum_k = dp_sum(dot(dkp, k, ((1,), (1,))).astype(BF16))
    grad_v = back_call(proj_value, dvp)
    grad_k = back_call(proj_key, dkp)
    return gq[None], grad_k[None], grad_v[None], sum_k, sum_v


def solution(mesh):
    block = P("dp", "seq", None)
    return jax.shard_map(
        body,
        mesh=mesh,
        in_specs=(block, block, block, block, P(None, "seq"), P(None, "seq")),
        out_specs=(block, block, block, P("dp", "seq"), P("dp", "seq")),
        check_vma=False,
    )
```
